512 devices in a mesh: grid: 64 (over x, y, core), layer: 8 (over z).
Axes of the slice: x: 4, y: 8, z: 8, core: 2. Of those that a mesh axis runs over, the one named last changes fastest.
Arguments:
- tensor_blocks: bfloat16 [32768, 64, 128], P(('grid', 'layer')), may hold values from -6 to 6
- tensor_screen: int32 [512, 2], P(('grid', 'layer')), may hold values 0 or 1
- density: bfloat16 [32768, 512], P(('grid', 'layer')), may hold values from -0.03125 to 0.03125
- density_screen: int32 [512, 8], P(('grid', 'layer')), may hold values 0 or 1
Outputs:
- contracted: bfloat16 [512, 64, 128], P(('grid', 'layer'))
The draws below stay inside these ranges and needn't reach their ends.
Inputs may be any that keep to these rules, and one draw needn't show every extreme that they name: `tensor_screen`: 1 where the pair of atom blocks survives screening, else 0. `density_screen`: 1 where the pair of atom blocks survives screening, else 0.
All inputs are finite; a program needn't handle non-finite values.
Results may differ from the reference program's by a relative error of at most 0.0022.
Values may be sent and summed in bfloat16 or wider, within the bound.
A program may use at most 64 MiB of HBM per device.

```python
import jax
import jax.numpy as jnp
from jax import lax

B = 64
MB = 2
CB = 8
NUB = 512
NNU = 32768
NP = 64
NMU = 128
NC = 512
N_GRID = 64
N_LAYER = 8


def place_ends(array, stream_key, least, high):
    longest = array.shape.index(max(array.shape))
    spots = []
    for shift in (0, 1):
        where = [jax.random.randint(jax.random.fold_in(stream_key, axis), (), 0, length) for axis, length in enumerate(array.shape)]
        where[longest] = (where[longest] + shift) % array.shape[longest]
        spots.append(tuple(where))
    return array.at[spots[0]].set(least).at[spots[1]].set(high)


def block_scale(stream_key, extent, cuts, smallest, high):
    def one(position, shards_of):
        heights = jax.random.uniform(jax.random.fold_in(jax.random.fold_in(stream_key, 6), position), (shards_of,), jnp.float32, smallest / len(cuts), high / len(cuts))
        return jnp.repeat(jnp.exp(heights), extent[position] // shards_of).reshape((-1,) + (1,) * (len(extent) - position - 1))

    level = one(*cuts[0])
    for cut in cuts[1:]:
        level = level * one(*cut)
    return level


def bell_draw(own_key, dims, scale, bound, split=(), kind=jnp.bfloat16):
    gain = block_scale(own_key, dims, split, -0.22, 0.18) if split else 1.0
    drawn = jax.random.normal(own_key, dims, jnp.float32) * scale * gain
    return jnp.minimum(jnp.maximum(drawn, -bound), bound).astype(kind)


def setup_inputs(seed: int = 0) -> dict:
    seeds = jax.random.split(jax.random.key(seed), 5)
    return {
        "tensor_blocks": bell_draw(seeds[0], (NNU, NP, NMU), 1.0, 6.0, ((0, 512),)),
        "tensor_screen": place_ends((jax.random.randint(seeds[1], (NUB, MB), 0, 4) < 3).astype(jnp.int32), jax.random.fold_in(seeds[1], 1), 0, 1),
        "density": bell_draw(seeds[2], (NNU, NC), NNU ** -0.5, 0.03125, ((0, 512),)),
        "density_screen": place_ends((jax.random.randint(seeds[3], (NUB, CB), 0, 4) < 3).astype(jnp.int32), jax.random.fold_in(seeds[3], 1), 0, 1),
    }


def reference(tensor_blocks, tensor_screen, density, density_screen):
    tensor_view = tensor_blocks.reshape(N_GRID * N_LAYER, B, NP, MB, B)
    screen_view = tensor_screen.reshape(N_GRID * N_LAYER, MB)
    density_view = density.reshape(N_GRID * N_LAYER, B, CB, B)
    dscreen_view = density_screen.reshape(N_GRID * N_LAYER, CB)
    flat_rows = NP * MB * B

    def add_block(running_sum, block_index):
        tensor_piece = tensor_view[block_index]
        tensor_mask = screen_view[block_index].astype(tensor_piece.dtype)
        kept_tensor = (tensor_piece * tensor_mask[None, None, :, None]).reshape(B, flat_rows)
        density_piece = density_view[block_index]
        density_mask = dscreen_view[block_index].astype(density_piece.dtype)
        kept_density = (density_piece * density_mask[None, :, None]).reshape(B, NC)
        update = lax.dot_general(kept_density, kept_tensor, (((0,), (0,)), ((), ())),
                                 preferred_element_type=jnp.float32)
        return running_sum + update, None

    start_sum = jnp.zeros((NC, flat_rows), jnp.float32)
    running_sum, _ = lax.scan(add_block, start_sum, jnp.arange(N_GRID * N_LAYER, dtype=jnp.int32))
    return running_sum.astype(jnp.bfloat16).reshape(NC, NP, NMU)
```

```python
import functools

import jax
import jax.numpy as jnp
from jax import lax
from jax.experimental import pallas as pl
from jax.experimental.pallas import tpu as pltpu
from jax.sharding import PartitionSpec as P

MESH = pl.DeviceIdType.MESH

NX, RING, CORES = 4, 8, 2
GROUP = NX * CORES
ROWS = 64
NAUX = 64
LANES = 128
NSIG = 512
CHUNKS = 4
PAIR = 2 * LANES
DEPTH = GROUP * ROWS
SLAB = GROUP * RING


def remote(src, dst, send_sem, recv_sem, device):
    return pltpu.make_async_remote_copy(
        src_ref=src, dst_ref=dst, send_sem=send_sem, recv_sem=recv_sem,
        device_id=device, device_id_type=MESH)


def kernel(tensor_hbm, tscreen, density_hbm, dscreen, out_ref,
           tb, tf, stage, recv_t, db, dall, perm, dt, part, near, mid, tie, far,
           first, recv_b, tiles, outgoing, fin,
           load_sem, own_sem, d_send, d_recv, t_send, t_recv,
           near_send, near_recv, mid_send, mid_recv, tie_send, tie_recv, far_send, far_recv,
           b_send, b_recv, f_send, f_recv):
    grid = lax.axis_index("grid")
    z = lax.axis_index("layer")
    core = lax.rem(grid, CORES)
    y = lax.rem(grid // CORES, RING)
    x = grid // (CORES * RING)
    me = x * CORES + core

    def at(x_, y_, core_, z_):
        return ((x_ * RING + y_) * CORES + core_, z_)

    def member(pos):
        return at(pos // CORES, y, lax.rem(pos, CORES), z)

    a = jnp.where(core == 0, y, z)
    b = jnp.where(core == 0, z, y)

    def on_a(i):
        return at(x, jnp.where(core == 0, i, y), core, jnp.where(core == 0, z, i))

    def on_b(i):
        return at(x, jnp.where(core == 0, y, i), core, jnp.where(core == 0, i, z))

    def ring(i):
        return lax.rem(i + 2 * RING, RING)

    load_t = pltpu.make_async_copy(tensor_hbm, tb, load_sem.at[0])
    load_d = pltpu.make_async_copy(density_hbm, db, load_sem.at[1])
    load_d.start()
    load_t.start()

    barrier = pltpu.get_barrier_semaphore()
    peers = [member(lax.rem(me + d, GROUP)) for d in range(1, GROUP)]
    peers += [on_a(ring(a + d)) for d in (1, 2, -1, -2)]
    peers += [on_b(ring(b + d)) for d in range(1, RING)]
    for peer in peers:
        pl.semaphore_signal(barrier, inc=1, device_id=peer, device_id_type=MESH)

    my_rows = pl.ds(pl.multiple_of(me * ROWS, ROWS), ROWS)
    lane = lax.broadcasted_iota(jnp.int32, (ROWS, LANES), 1)
    load_d.wait()
    for t in range(NSIG // LANES):
        cols = pl.ds(t * LANES, LANES)
        low = dscreen[0, 2 * t].astype(jnp.float32)
        high = dscreen[0, 2 * t + 1].astype(jnp.float32)
        keep = jnp.where(lane < 64, low, high)
        dall[my_rows, cols] = (db[:, cols].astype(jnp.float32) * keep).astype(jnp.bfloat16)

    keep_t = jnp.where(lane < 64, tscreen[0, 0].astype(jnp.float32), tscreen[0, 1].astype(jnp.float32))
    load_t.wait()

    @pl.loop(0, ROWS, unroll=8)
    def _(n):
        tf[pl.ds(pl.multiple_of(n * NAUX, NAUX), NAUX), :] = tb[n].astype(jnp.float32) * keep_t

    def regroup(c):
        for pos in range(GROUP):
            for h in range(2):
                p = pos * 8 + 2 * c + h
                rows = tf[pl.ds(p, ROWS, stride=NAUX), :]
                stage[c, pos, :, h * LANES:(h + 1) * LANES] = rows.astype(jnp.bfloat16)

    regroup(0)
    pl.semaphore_wait(barrier, len(peers))

    other = at(x, y, 1 - core, z)
    d_copies = []
    for d in range(1, NX):
        peer = at(lax.rem(x + d, NX), y, core, z)
        d_copies.append(remote(dall.at[my_rows], dall.at[my_rows], d_send.at[d - 1], d_recv.at[d - 1], peer))
    d_copies.append(remote(dall.at[my_rows], dall.at[my_rows], d_send.at[3], d_recv.at[3], other))
    for copy in d_copies:
        copy.start()

    t_copies = {}

    def send_t(c):
        for d in range(1, GROUP):
            pos = lax.rem(me + d, GROUP)
            copy = remote(stage.at[c, pos], recv_t.at[c, my_rows], t_send.at[c, d - 1], t_recv.at[c, d - 1],
                          member(pos))
            copy.start()
            t_copies[c, d] = copy
        own = pltpu.make_async_copy(stage.at[c, me], recv_t.at[c, my_rows], own_sem.at[c])
        own.start()
        t_copies[c, 0] = own

    send_t(0)
    for c in range(1, CHUNKS):
        regroup(c)
        send_t(c)

    row = lax.broadcasted_iota(jnp.int32, (SLAB, NSIG), 0)
    col = lax.broadcasted_iota(jnp.int32, (SLAB, NSIG), 1)
    j = row & 7
    for block in range(RING):
        y_ = jnp.where(core == 0, block, row >> 3)
        z_ = jnp.where(core == 0, row >> 3, block)
        sigma = (j >> 1) * 128 + y_ * 16 + (j & 1) * 8 + z_
        perm[block * SLAB:(block + 1) * SLAB, :] = jnp.where(sigma == col, 1.0, 0.0).astype(jnp.bfloat16)

    relays = []
    for d in range(1, NX):
        d_copies[d - 1].wait_recv()
        src = lax.rem(x + NX - d, NX) * CORES + core
        rows = pl.ds(pl.multiple_of(src * ROWS, ROWS), ROWS)
        copy = remote(dall.at[rows], dall.at[rows], d_send.at[3 + d], d_recv.at[3 + d], other)
        copy.start()
        relays.append(copy)
    d_copies[3].wait_recv()
    for copy in relays:
        copy.wait_recv()
    dt[...] = lax.dot_general(perm[...], dall[...], (((1,), (1,)), ((), ())),
                              preferred_element_type=jnp.float32).astype(jnp.bfloat16)

    def slab(c, i):
        return part.at[c, pl.ds(pl.multiple_of(ring(i) * SLAB, SLAB), SLAB)]

    started = []

    def go(copy):
        copy.start()
        started.append(copy)
        return copy

    near_c, mid_c, tie_c, far_c, b_c = {}, {}, {}, {}, {}

    def multiply(c):
        t_copies[c, 0].wait()
        for d in range(1, GROUP):
            t_copies[c, d].wait_recv()
        part[c] = jnp.dot(dt[...], recv_t[c], preferred_element_type=jnp.float32)
        for k, step in enumerate((1, -1)):
            to = on_a(ring(a + step))
            mid_c[c, k] = go(remote(slab(c, a + 3 * step), mid.at[c, k], mid_send.at[c, k], mid_recv.at[c, k], to))
        step = -2 if c % 2 == 0 else 2
        tie_c[c] = go(remote(slab(c, a + 4), tie.at[c], tie_send.at[c], tie_recv.at[c], on_a(ring(a + step))))
        for k, step in enumerate((1, -1)):
            to = on_a(ring(a + step))
            near_c[c, k] = go(remote(slab(c, a + step), near.at[c, k], near_send.at[c, k], near_recv.at[c, k], to))

    def forward(c):
        for k, step in enumerate((2, -2)):
            mid_c[c, k].wait_recv()
            with_tie = k == (1 if c % 2 == 0 else 0)
            if with_tie:
                tie_c[c].wait_recv()
            mine = slab(c, a + step)
            total = mine[...] + mid[c, k]
            if with_tie:
                total = total + tie[c]
            mine[...] = total
            far_c[c, k] = go(remote(mine, far.at[c, k], far_send.at[c, k], far_recv.at[c, k],
                                    on_a(ring(a + step))))

    def reduce_a(c):
        for k in range(2):
            near_c[c, k].wait_recv()
            far_c[c, k].wait_recv()
        first[c] = (slab(c, a)[...] + near[c, 0]) + near[c, 1] + (far[c, 0] + far[c, 1])
        for d in range(1, RING):
            to = ring(b + d)
            rows = pl.ds(pl.multiple_of(to * GROUP, GROUP), GROUP)
            b_c[c, d] = go(remote(first.at[c, rows], recv_b.at[c, d - 1], b_send.at[c, d - 1],
                                  b_recv.at[c, d - 1], on_b(to)))

    def reduce_b(c):
        rows = pl.ds(pl.multiple_of(b * GROUP, GROUP), GROUP)
        total = first[c, rows, :]
        for d in range(1, RING):
            b_c[c, d].wait_recv()
            total = total + recv_b[c, d - 1]
        for h in range(2):
            p = 2 * c + h
            tiles[p * GROUP:(p + 1) * GROUP, :] = total[:, h * LANES:(h + 1) * LANES]

    multiply(0)
    multiply(1)
    forward(0)
    multiply(2)
    forward(1)
    reduce_a(0)
    multiply(3)
    forward(2)
    reduce_a(1)
    forward(3)
    reduce_a(2)
    reduce_b(0)
    reduce_a(3)
    for c in range(1, CHUNKS):
        reduce_b(c)

    for k in range(GROUP):
        outgoing[k] = tiles[pl.ds(k, 8, stride=GROUP), :]
    my_p = pl.ds(pl.multiple_of(me * 8, 8), 8)
    f_c = []
    for d in range(1, GROUP):
        pos = lax.rem(me + d, GROUP)
        f_c.append(go(remote(outgoing.at[pos], fin.at[my_p], f_send.at[d - 1], f_recv.at[d - 1], member(pos))))
    fin[my_p, :] = outgoing[me]
    for copy in f_c:
        copy.wait_recv()
    out_ref[...] = fin[...].astype(jnp.bfloat16)

    for copy in d_copies + relays + started:
        copy.wait_send()
    for c in range(CHUNKS):
        for d in range(1, GROUP):
            t_copies[c, d].wait_send()


def body(tensor_blocks, tensor_screen, density, density_screen):
    dma = pltpu.SemaphoreType.DMA
    out = pl.pallas_call(
        kernel,
        out_shape=jax.ShapeDtypeStruct((NAUX, LANES), jnp.bfloat16),
        in_specs=[
            pl.BlockSpec(memory_space=pl.ANY),
            pl.BlockSpec(memory_space=pltpu.SMEM),
            pl.BlockSpec(memory_space=pl.ANY),
            pl.BlockSpec(memory_space=pltpu.SMEM),
        ],
        out_specs=pl.BlockSpec(memory_space=pltpu.VMEM),
        scratch_shapes=[
            pltpu.VMEM((ROWS, NAUX, LANES), jnp.bfloat16),
            pltpu.VMEM((ROWS * NAUX, LANES), jnp.float32),
            pltpu.VMEM((CHUNKS, GROUP, ROWS, PAIR), jnp.bfloat16),
            pltpu.VMEM((CHUNKS, DEPTH, PAIR), jnp.bfloat16),
            pltpu.VMEM((ROWS, NSIG), jnp.bfloat16),
            pltpu.VMEM((DEPTH, NSIG), jnp.bfloat16),
            pltpu.VMEM((NSIG, NSIG), jnp.bfloat16),
            pltpu.VMEM((NSIG, DEPTH), jnp.bfloat16),
            pltpu.VMEM((CHUNKS, NSIG, PAIR), jnp.float32),
            pltpu.VMEM((CHUNKS, 2, SLAB, PAIR), jnp.float32),
            pltpu.VMEM((CHUNKS, 2, SLAB, PAIR), jnp.float32),
            pltpu.VMEM((CHUNKS, SLAB, PAIR), jnp.float32),
            pltpu.VMEM((CHUNKS, 2, SLAB, PAIR), jnp.float32),
            pltpu.VMEM((CHUNKS, SLAB, PAIR), jnp.float32),
            pltpu.VMEM((CHUNKS, RING - 1, GROUP, PAIR), jnp.float32),
            pltpu.VMEM((8 * GROUP, LANES), jnp.float32),
            pltpu.VMEM((GROUP, 8, LANES), jnp.float32),
            pltpu.VMEM((NAUX, LANES), jnp.float32),
            dma((2,)), dma((CHUNKS,)),
            dma((7,)), dma((7,)),
            dma((CHUNKS, 7)), dma((CHUNKS, 7)),
            dma((CHUNKS, 2)), dma((CHUNKS, 2)),
            dma((CHUNKS, 2)), dma((CHUNKS, 2)),
            dma((CHUNKS,)), dma((CHUNKS,)),
            dma((CHUNKS, 2)), dma((CHUNKS, 2)),
            dma((CHUNKS, 7)), dma((CHUNKS, 7)),
            dma((7,)), dma((7,)),
        ],
        compiler_params=pltpu.CompilerParams(
            collective_id=0, has_side_effects=True, vmem_limit_bytes=40 << 20),
        name="contract",
    )(tensor_blocks, tensor_screen, density, density_screen)
    return out.reshape(1, NAUX, LANES)


def solution(mesh):
    in_specs = (
        P(("grid", "layer"), None, None),
        P(("grid", "layer"), None),
        P(("grid", "layer"), None),
        P(("grid", "layer"), None),
    )
    out_specs = P(("grid", "layer"), None, None)
    return jax.shard_map(body, mesh=mesh, in_specs=in_specs, out_specs=out_specs, check_vma=False)
```

```python
import jax
import jax.numpy as jnp
from jax import lax
from jax.experimental import pallas as pl
from jax.experimental.pallas import tpu as pltpu
from jax.sharding import PartitionSpec as P

MESH = pl.DeviceIdType.MESH

NX, RING, CORES = 4, 8, 2
GROUP = NX * CORES
ROWS = 64
NAUX = 64
LANES = 128
NSIG = 512
SLICES = 4
WIDE = NAUX // SLICES
SHARE = NAUX // GROUP * LANES
PARTS = tuple((q, 1) for q in range(8))
AHEAD = 3
DEPTH = GROUP * ROWS
SLAB = GROUP * RING


def remote(src, dst, send_sem, recv_sem, device):
    return pltpu.make_async_remote_copy(
        src_ref=src, dst_ref=dst, send_sem=send_sem, recv_sem=recv_sem,
        device_id=device, device_id_type=MESH)


def kernel(tensor_hbm, tscreen_hbm, density_hbm, dscreen_hbm, out_ref,
           tscreen, dscreen, tb, tf, stage, recv_t, db, dall, perm, dt, part, near, mid, tie, far,
           first, recv_b, tiles, outgoing, fin, ordered,
           load_sem, own_sem, d_send, d_recv, t_send, t_recv,
           near_send, near_recv, mid_send, mid_recv, tie_send, tie_recv, far_send, far_recv,
           b_send, b_recv, f_send, f_recv, hello_a, hello_b, hello_far):
    grid = lax.axis_index("grid")
    z = lax.axis_index("layer")
    core = lax.rem(grid, CORES)
    y = lax.rem(grid // CORES, RING)
    x = grid // (CORES * RING)
    me = x * CORES + core

    def at(x_, y_, core_, z_):
        return ((x_ * RING + y_) * CORES + core_, z_)

    def member(pos):
        return at(pos // CORES, y, lax.rem(pos, CORES), z)

    a = jnp.where(core == 0, y, z)
    b = jnp.where(core == 0, z, y)

    def on_a(i):
        return at(x, jnp.where(core == 0, i, y), core, jnp.where(core == 0, z, i))

    def on_b(i):
        return at(x, jnp.where(core == 0, y, i), core, jnp.where(core == 0, i, z))

    def ring(i):
        return lax.rem(i + 2 * RING, RING)

    def greet(sem, peers):
        for peer in peers:
            pl.semaphore_signal(sem, inc=1, device_id=peer, device_id_type=MESH)

    load_screens = (pltpu.make_async_copy(dscreen_hbm, dscreen, load_sem.at[SLICES]),
                    pltpu.make_async_copy(tscreen_hbm, tscreen, load_sem.at[SLICES + 1]))
    load_d = pltpu.make_async_copy(density_hbm, db, load_sem.at[SLICES + 2])
    load_t = [pltpu.make_async_copy(tensor_hbm.at[:, pl.ds(c * WIDE, WIDE), :], tb.at[c], load_sem.at[c])
              for c in range(SLICES)]
    for copy in (*load_screens, load_d, *load_t):
        copy.start()

    near_a = [on_a(ring(a + 1)), on_a(ring(a - 1))]
    near_b = [on_b(ring(b + 1)), on_b(ring(b - 1))]
    far_b = [on_b(ring(b + 2)), on_b(ring(b - 2))]
    barrier = pltpu.get_barrier_semaphore()
    peers = [member(lax.rem(me + d, GROUP)) for d in range(1, GROUP)] + near_a + near_b
    greet(barrier, peers)

    my_rows = pl.ds(pl.multiple_of(me * ROWS, ROWS), ROWS)
    lane = lax.broadcasted_iota(jnp.int32, (ROWS, LANES), 1)
    load_screens[0].wait()
    load_screens[1].wait()
    load_d.wait()
    for t in range(NSIG // LANES):
        cols = pl.ds(t * LANES, LANES)
        low = dscreen[0, 2 * t].astype(jnp.float32)
        high = dscreen[0, 2 * t + 1].astype(jnp.float32)
        keep = jnp.where(lane < 64, low, high)
        dall[my_rows, cols] = (db[:, cols].astype(jnp.float32) * keep).astype(jnp.bfloat16)

    lane = lax.broadcasted_iota(jnp.int32, (WIDE, LANES), 1)
    keep_t = jnp.where(lane < 64, tscreen[0, 0].astype(jnp.float32), tscreen[0, 1].astype(jnp.float32))

    def regroup(c):
        load_t[c].wait()

        @pl.loop(0, ROWS, unroll=16)
        def _(n):
            tf[c, pl.ds(pl.multiple_of(n * WIDE, WIDE), WIDE), :] = tb[c, n].astype(jnp.float32) * keep_t

        for pos in range(GROUP):
            for h in range(2):
                rows = tf[c, pl.ds(2 * pos + h, ROWS, stride=WIDE), :]
                q = 2 * c + h
                stage[pos, :, q * LANES:(q + 1) * LANES] = rows.astype(jnp.bfloat16)

    regroup(0)
    pl.semaphore_wait(barrier, len(peers))

    other = at(x, y, 1 - core, z)
    d_copies = []
    for d in range(1, NX):
        peer = at(lax.rem(x + d, NX), y, core, z)
        d_copies.append(remote(dall.at[my_rows], dall.at[my_rows], d_send.at[d - 1], d_recv.at[d - 1], peer))
    d_copies.append(remote(dall.at[my_rows], dall.at[my_rows], d_send.at[3], d_recv.at[3], other))
    for copy in d_copies:
        copy.start()

    def span(i):
        q, count = PARTS[i]
        return pl.ds(q * LANES, count * LANES)

    t_copies = {}

    def send_t(i):
        cols = span(i)
        for d in range(1, GROUP):
            pos = lax.rem(me + d, GROUP)
            copy = remote(stage.at[pos, :, cols], recv_t.at[my_rows, cols], t_send.at[i, d - 1],
                          t_recv.at[i, d - 1], member(pos))
            copy.start()
            t_copies[i, d] = copy
        own = pltpu.make_async_copy(stage.at[me, :, cols], recv_t.at[my_rows, cols], own_sem.at[i])
        own.start()
        t_copies[i, 0] = own

    for i in range(2):
        send_t(i)
    greet(hello_a, near_a)
    greet(hello_b, near_b)
    for c in range(1, SLICES):
        regroup(c)

    relays = []
    for d in range(1, NX):
        d_copies[d - 1].wait_recv()
        src = lax.rem(x + NX - d, NX) * CORES + core
        rows = pl.ds(pl.multiple_of(src * ROWS, ROWS), ROWS)
        copy = remote(dall.at[rows], dall.at[rows], d_send.at[3 + d], d_recv.at[3 + d], other)
        copy.start()
        relays.append(copy)
    for i in range(2, AHEAD):
        send_t(i)

    row = lax.broadcasted_iota(jnp.int32, (SLAB, NSIG), 0)
    col = lax.broadcasted_iota(jnp.int32, (SLAB, NSIG), 1)
    j = row & 7
    for block in range(RING):
        y_ = jnp.where(core == 0, block, row >> 3)
        z_ = jnp.where(core == 0, row >> 3, block)
        sigma = (j >> 1) * 128 + y_ * 16 + (j & 1) * 8 + z_
        perm[block * SLAB:(block + 1) * SLAB, :] = jnp.where(sigma == col, 1.0, 0.0).astype(jnp.bfloat16)

    d_copies[3].wait_recv()
    for copy in relays:
        copy.wait_recv()
    dt[...] = lax.dot_general(perm[...], dall[...], (((1,), (1,)), ((), ())),
                              preferred_element_type=jnp.float32).astype(jnp.bfloat16)

    def slab(i, index):
        return part.at[pl.ds(pl.multiple_of(ring(index) * SLAB, SLAB), SLAB), span(i)]

    started = []

    def go(copy):
        copy.start()
        started.append(copy)
        return copy

    near_c, mid_c, tie_c, far_c, b_c = {}, {}, {}, {}, {}

    def multiply(i):
        cols = span(i)
        t_copies[i, 0].wait()
        for d in range(1, GROUP):
            t_copies[i, d].wait_recv()
        if i + AHEAD < len(PARTS):
            send_t(i + AHEAD)
        part[:, cols] = jnp.dot(dt[...], recv_t[:, cols], preferred_element_type=jnp.float32)
        for k, step in enumerate((1, -1)):
            to = on_a(ring(a + step))
            mid_c[i, k] = go(remote(slab(i, a + 3 * step), mid.at[k, :, cols], mid_send.at[i, k],
                                    mid_recv.at[i, k], to))
        if i == 0:
            pl.semaphore_wait(hello_a, 2)
            pl.semaphore_wait(hello_b, 2)
            greet(hello_far, far_b)
        step = -2 if i % 2 == 0 else 2
        tie_c[i] = go(remote(slab(i, a + 4), tie.at[:, cols], tie_send.at[i], tie_recv.at[i],
                             on_a(ring(a + step))))
        for k, step in enumerate((1, -1)):
            to = on_a(ring(a + step))
            near_c[i, k] = go(remote(slab(i, a + step), near.at[k, :, cols], near_send.at[i, k],
                                     near_recv.at[i, k], to))

    def forward(i):
        cols = span(i)
        for k, step in enumerate((2, -2)):
            mid_c[i, k].wait_recv()
            with_tie = k == (1 if i % 2 == 0 else 0)
            if with_tie:
                tie_c[i].wait_recv()
            mine = slab(i, a + step)
            total = mine[...] + mid[k, :, cols]
            if with_tie:
                total = total + tie[:, cols]
            mine[...] = total
            far_c[i, k] = go(remote(mine, far.at[k, :, cols], far_send.at[i, k], far_recv.at[i, k],
                                    on_a(ring(a + step))))

    def reduce_a(i):
        cols = span(i)
        for k in range(2):
            near_c[i, k].wait_recv()
            far_c[i, k].wait_recv()
        first[:, cols] = (slab(i, a)[...] + near[0, :, cols]) + near[1, :, cols] + (far[0, :, cols] + far[1, :, cols])
        if i == 0:
            pl.semaphore_wait(hello_far, 2)
        for d in range(1, RING):
            to = ring(b + d)
            rows = pl.ds(pl.multiple_of(to * GROUP, GROUP), GROUP)
            b_c[i, d] = go(remote(first.at[rows, cols], recv_b.at[d - 1, :, cols], b_send.at[i, d - 1],
                                  b_recv.at[i, d - 1], on_b(to)))

    def reduce_b(i):
        q, count = PARTS[i]
        rows = pl.ds(pl.multiple_of(b * GROUP, GROUP), GROUP)
        total = first[rows, span(i)]
        for d in range(1, RING):
            b_c[i, d].wait_recv()
            total = total + recv_b[d - 1, :, span(i)]
        for h in range(count):
            tiles[(q + h) * GROUP:(q + h + 1) * GROUP, :] = total[:, h * LANES:(h + 1) * LANES]

    last = len(PARTS)
    for step in range(last + 6):
        if step < last:
            multiply(step)
        if 0 <= step - 2 < last:
            forward(step - 2)
        if 0 <= step - 4 < last:
            reduce_a(step - 4)
        if 0 <= step - 6 < last:
            reduce_b(step - 6)

    for k in range(GROUP):
        outgoing[k] = tiles[pl.ds(k, 8, stride=GROUP), :]
    mine = pl.ds(pl.multiple_of(me * 8, 8), 8)
    f_c = []
    for d in range(1, GROUP):
        pos = lax.rem(me + d, GROUP)
        copy = remote(outgoing.at[pos], fin.at[mine], f_send.at[d - 1], f_recv.at[d - 1], member(pos))
        copy.start()
        f_c.append(copy)
    fin[mine, :] = outgoing[me]
    for copy in d_copies + relays + started:
        copy.wait_send()
    for i in range(last):
        for d in range(1, GROUP):
            t_copies[i, d].wait_send()
    for copy in f_c:
        copy.wait()
    for q in range(8):
        ordered[pl.ds(WIDE * (q // 2) + q % 2, GROUP, stride=2), :] = fin[pl.ds(q, GROUP, stride=8), :]
    out_ref[...] = ordered[...].astype(jnp.bfloat16)


def body(tensor_blocks, tensor_screen, density, density_screen):
    dma = pltpu.SemaphoreType.DMA
    regular = pltpu.SemaphoreType.REGULAR
    parts = len(PARTS)
    out = pl.pallas_call(
        kernel,
        out_shape=jax.ShapeDtypeStruct((NAUX, LANES), jnp.bfloat16),
        in_specs=[pl.BlockSpec(memory_space=pltpu.HBM)] * 4,
        out_specs=pl.BlockSpec(memory_space=pltpu.VMEM),
        scratch_shapes=[
            pltpu.SMEM((1, 2), jnp.int32),
            pltpu.SMEM((1, 8), jnp.int32),
            pltpu.VMEM((SLICES, ROWS, WIDE, LANES), jnp.bfloat16),
            pltpu.VMEM((SLICES, ROWS * WIDE, LANES), jnp.float32),
            pltpu.VMEM((GROUP, ROWS, SHARE), jnp.bfloat16),
            pltpu.VMEM((DEPTH, SHARE), jnp.bfloat16),
            pltpu.VMEM((ROWS, NSIG), jnp.bfloat16),
            pltpu.VMEM((DEPTH, NSIG), jnp.bfloat16),
            pltpu.VMEM((NSIG, NSIG), jnp.bfloat16),
            pltpu.VMEM((NSIG, DEPTH), jnp.bfloat16),
            pltpu.VMEM((NSIG, SHARE), jnp.float32),
            pltpu.VMEM((2, SLAB, SHARE), jnp.float32),
            pltpu.VMEM((2, SLAB, SHARE), jnp.float32),
            pltpu.VMEM((SLAB, SHARE), jnp.float32),
            pltpu.VMEM((2, SLAB, SHARE), jnp.float32),
            pltpu.VMEM((SLAB, SHARE), jnp.float32),
            pltpu.VMEM((RING - 1, GROUP, SHARE), jnp.float32),
            pltpu.VMEM((8 * GROUP, LANES), jnp.float32),
            pltpu.VMEM((GROUP, 8, LANES), jnp.float32),
            pltpu.VMEM((NAUX, LANES), jnp.float32),
            pltpu.VMEM((NAUX, LANES), jnp.float32),
            dma((SLICES + 3,)), dma((parts,)),
            dma((7,)), dma((7,)),
            dma((parts, 7)), dma((parts, 7)),
            dma((parts, 2)), dma((parts, 2)),
            dma((parts, 2)), dma((parts, 2)),
            dma((parts,)), dma((parts,)),
            dma((parts, 2)), dma((parts, 2)),
            dma((parts, 7)), dma((parts, 7)),
            dma((7,)), dma((7,)),
            regular, regular, regular,
        ],
        compiler_params=pltpu.CompilerParams(
            collective_id=0, has_side_effects=True, vmem_limit_bytes=40 << 20),
        name="contract",
    )(*(pltpu.with_memory_space_constraint(v, pltpu.HBM)
        for v in (tensor_blocks, tensor_screen, density, density_screen)))
    return out.reshape(1, NAUX, LANES)


def solution(mesh):
    in_specs = (
        P(("grid", "layer"), None, None),
        P(("grid", "layer"), None),
        P(("grid", "layer"), None),
        P(("grid", "layer"), None),
    )
    out_specs = P(("grid", "layer"), None, None)
    return jax.shard_map(body, mesh=mesh, in_specs=in_specs, out_specs=out_specs, check_vma=False)
```

```python
import jax
import jax.numpy as jnp
from jax import lax
from jax.experimental import pallas as pl
from jax.experimental.pallas import tpu as pltpu
from jax.sharding import PartitionSpec as P

MESH = pl.DeviceIdType.MESH

NX, RING, CORES = 4, 8, 2
GROUP = NX * CORES
ROWS = 64
NAUX = 64
LANES = 128
NSIG = 512
SLICES = 4
WIDE = NAUX // SLICES
SHARE = NAUX // GROUP * LANES
PARTS = tuple((q, 1) for q in range(8))
STEPS = 32000.0
TINY = 1e-33
AHEAD = 4
DEPTH = GROUP * ROWS
SLAB = GROUP * RING


def remote(src, dst, send_sem, recv_sem, device):
    return pltpu.make_async_remote_copy(
        src_ref=src, dst_ref=dst, send_sem=send_sem, recv_sem=recv_sem,
        device_id=device, device_id_type=MESH)


def kernel(tensor_hbm, tscreen_hbm, density_hbm, dscreen_hbm, out_ref,
           tscreen, dscreen, tb, tf, stage, recv_t, db, dall, perm, dt, part, coded, unit, near, units,
           first, recv_b, tiles, outgoing, fin, ordered,
           load_sem, own_sem, d_send, d_recv, t_send, t_recv,
           near_send, near_recv, unit_send, unit_recv,
           b_send, b_recv, f_send, f_recv, hello_a, hello_b, hello_far):
    grid = lax.axis_index("grid")
    z = lax.axis_index("layer")
    core = lax.rem(grid, CORES)
    y = lax.rem(grid // CORES, RING)
    x = grid // (CORES * RING)
    me = x * CORES + core

    def at(x_, y_, core_, z_):
        return ((x_ * RING + y_) * CORES + core_, z_)

    def member(pos):
        return at(pos // CORES, y, lax.rem(pos, CORES), z)

    a = jnp.where(core == 0, y, z)
    b = jnp.where(core == 0, z, y)

    def on_a(i):
        return at(x, jnp.where(core == 0, i, y), core, jnp.where(core == 0, z, i))

    def on_b(i):
        return at(x, jnp.where(core == 0, y, i), core, jnp.where(core == 0, i, z))

    def ring(i):
        return lax.rem(i + 2 * RING, RING)

    def greet(sem, peers):
        for peer in peers:
            pl.semaphore_signal(sem, inc=1, device_id=peer, device_id_type=MESH)

    load_screens = (pltpu.make_async_copy(dscreen_hbm, dscreen, load_sem.at[SLICES]),
                    pltpu.make_async_copy(tscreen_hbm, tscreen, load_sem.at[SLICES + 1]))
    load_d = pltpu.make_async_copy(density_hbm, db, load_sem.at[SLICES + 2])
    load_t = [pltpu.make_async_copy(tensor_hbm.at[:, pl.ds(c * WIDE, WIDE), :], tb.at[c], load_sem.at[c])
              for c in range(SLICES)]
    for copy in (*load_screens, load_d, *load_t):
        copy.start()

    near_a = [on_a(ring(a + 1)), on_a(ring(a - 1))]
    near_b = [on_b(ring(b + 1)), on_b(ring(b - 1))]
    far_a = [on_a(ring(a + 2)), on_a(ring(a - 2))]
    far_b = [on_b(ring(b + 2)), on_b(ring(b - 2))]
    barrier = pltpu.get_barrier_semaphore()
    peers = [member(lax.rem(me + d, GROUP)) for d in range(1, GROUP)] + near_a + near_b
    greet(barrier, peers)

    my_rows = pl.ds(pl.multiple_of(me * ROWS, ROWS), ROWS)
    lane = lax.broadcasted_iota(jnp.int32, (ROWS, LANES), 1)
    load_screens[0].wait()
    load_screens[1].wait()
    load_d.wait()
    for t in range(NSIG // LANES):
        cols = pl.ds(t * LANES, LANES)
        low = dscreen[0, 2 * t].astype(jnp.float32)
        high = dscreen[0, 2 * t + 1].astype(jnp.float32)
        keep = jnp.where(lane < 64, low, high)
        dall[my_rows, cols] = (db[:, cols].astype(jnp.float32) * keep).astype(jnp.bfloat16)

    lane = lax.broadcasted_iota(jnp.int32, (WIDE, LANES), 1)
    keep_t = jnp.where(lane < 64, tscreen[0, 0].astype(jnp.float32), tscreen[0, 1].astype(jnp.float32))

    def regroup(c):
        load_t[c].wait()

        @pl.loop(0, ROWS, unroll=16)
        def _(n):
            tf[c, pl.ds(pl.multiple_of(n * WIDE, WIDE), WIDE), :] = tb[c, n].astype(jnp.float32) * keep_t

        for pos in range(GROUP):
            for h in range(2):
                rows = tf[c, pl.ds(2 * pos + h, ROWS, stride=WIDE), :]
                q = 2 * c + h
                stage[pos, :, q * LANES:(q + 1) * LANES] = rows.astype(jnp.bfloat16)

    regroup(0)
    pl.semaphore_wait(barrier, len(peers))

    other = at(x, y, 1 - core, z)
    d_copies = []
    for d in range(1, NX):
        peer = at(lax.rem(x + d, NX), y, core, z)
        d_copies.append(remote(dall.at[my_rows], dall.at[my_rows], d_send.at[d - 1], d_recv.at[d - 1], peer))
    d_copies.append(remote(dall.at[my_rows], dall.at[my_rows], d_send.at[3], d_recv.at[3], other))
    for copy in d_copies:
        copy.start()

    def span(i):
        q, count = PARTS[i]
        return pl.ds(q * LANES, count * LANES)

    t_copies = {}

    def send_t(i):
        cols = span(i)
        for d in range(1, GROUP):
            pos = lax.rem(me + d, GROUP)
            copy = remote(stage.at[pos, :, cols], recv_t.at[my_rows, cols], t_send.at[i, d - 1],
                          t_recv.at[i, d - 1], member(pos))
            copy.start()
            t_copies[i, d] = copy
        own = pltpu.make_async_copy(stage.at[me, :, cols], recv_t.at[my_rows, cols], own_sem.at[i])
        own.start()
        t_copies[i, 0] = own

    for i in range(2):
        send_t(i)
    greet(hello_a, near_a)
    greet(hello_b, near_b)
    for c in range(1, SLICES):
        regroup(c)

    relays = []
    for d in range(1, NX):
        d_copies[d - 1].wait_recv()
        src = lax.rem(x + NX - d, NX) * CORES + core
        rows = pl.ds(pl.multiple_of(src * ROWS, ROWS), ROWS)
        copy = remote(dall.at[rows], dall.at[rows], d_send.at[3 + d], d_recv.at[3 + d], other)
        copy.start()
        relays.append(copy)
    for i in range(2, AHEAD):
        send_t(i)

    row = lax.broadcasted_iota(jnp.int32, (SLAB, NSIG), 0)
    col = lax.broadcasted_iota(jnp.int32, (SLAB, NSIG), 1)
    j = row & 7
    for block in range(RING):
        y_ = jnp.where(core == 0, block, row >> 3)
        z_ = jnp.where(core == 0, row >> 3, block)
        sigma = (j >> 1) * 128 + y_ * 16 + (j & 1) * 8 + z_
        perm[block * SLAB:(block + 1) * SLAB, :] = jnp.where(sigma == col, 1.0, 0.0).astype(jnp.bfloat16)

    d_copies[3].wait_recv()
    for copy in relays:
        copy.wait_recv()
    dt[...] = lax.dot_general(perm[...], dall[...], (((1,), (1,)), ((), ())),
                              preferred_element_type=jnp.float32).astype(jnp.bfloat16)

    def slab(ref, i, index):
        return ref.at[pl.ds(pl.multiple_of(ring(index) * SLAB, SLAB), SLAB), span(i)]

    started = []

    def go(copy):
        copy.start()
        started.append(copy)
        return copy

    near_c, unit_c, b_c = {}, {}, {}

    def multiply(i):
        cols = span(i)
        t_copies[i, 0].wait()
        for d in range(1, GROUP):
            t_copies[i, d].wait_recv()
        if i + AHEAD < len(PARTS):
            send_t(i + AHEAD)
        sums = jnp.dot(dt[...], recv_t[:, cols], preferred_element_type=jnp.float32)
        part[:, cols] = sums
        largest = jnp.maximum(jnp.max(jnp.abs(sums), axis=0, keepdims=True), TINY)
        unit[i] = largest * (1.0 / STEPS)
        coded[:, cols] = jnp.round(sums * (STEPS / largest)).astype(jnp.int32).astype(jnp.int16)
        if i == 0:
            pl.semaphore_wait(hello_a, 2)
            pl.semaphore_wait(hello_b, 2)
            greet(hello_far, far_b + far_a)
            pl.semaphore_wait(hello_far, 4)
        for d in (4, 3, 5, 2, 6, 1, 7):
            unit_c[i, d] = go(remote(unit.at[i], units.at[d - 1, i], unit_send.at[i, d - 1],
                                     unit_recv.at[i, d - 1], on_a(ring(a + d))))
            near_c[i, d] = go(remote(slab(coded, i, a + d), near.at[d - 1, :, cols], near_send.at[i, d - 1],
                                     near_recv.at[i, d - 1], on_a(ring(a + d))))

    def reduce_a(i):
        cols = span(i)
        total = slab(part, i, a)[...]
        for d in range(1, RING):
            near_c[i, d].wait_recv()
            unit_c[i, d].wait_recv()
            total = total + near[d - 1, :, cols].astype(jnp.int32).astype(jnp.float32) * units[d - 1, i]
        first[:, cols] = total
        for d in range(1, RING):
            to = ring(b + d)
            rows = pl.ds(pl.multiple_of(to * GROUP, GROUP), GROUP)
            b_c[i, d] = go(remote(first.at[rows, cols], recv_b.at[d - 1, :, cols], b_send.at[i, d - 1],
                                  b_recv.at[i, d - 1], on_b(to)))

    def reduce_b(i):
        q, count = PARTS[i]
        rows = pl.ds(pl.multiple_of(b * GROUP, GROUP), GROUP)
        total = first[rows, span(i)]
        for d in range(1, RING):
            b_c[i, d].wait_recv()
            total = total + recv_b[d - 1, :, span(i)]
        for h in range(count):
            tiles[(q + h) * GROUP:(q + h + 1) * GROUP, :] = total[:, h * LANES:(h + 1) * LANES]

    last = len(PARTS)
    for step in range(last + 8):
        if step < last:
            multiply(step)
        if 0 <= step - 4 < last:
            reduce_a(step - 4)
        if 0 <= step - 8 < last:
            reduce_b(step - 8)

    for k in range(GROUP):
        outgoing[k] = tiles[pl.ds(k, 8, stride=GROUP), :]
    mine = pl.ds(pl.multiple_of(me * 8, 8), 8)
    f_c = []
    for d in range(1, GROUP):
        pos = lax.rem(me + d, GROUP)
        copy = remote(outgoing.at[pos], fin.at[mine], f_send.at[d - 1], f_recv.at[d - 1], member(pos))
        copy.start()
        f_c.append(copy)
    fin[mine, :] = outgoing[me]
    for copy in d_copies + relays + started:
        copy.wait_send()
    for i in range(last):
        for d in range(1, GROUP):
            t_copies[i, d].wait_send()
    for copy in f_c:
        copy.wait()
    for q in range(8):
        ordered[pl.ds(WIDE * (q // 2) + q % 2, GROUP, stride=2), :] = fin[pl.ds(q, GROUP, stride=8), :]
    out_ref[...] = ordered[...].astype(jnp.bfloat16)


def body(tensor_blocks, tensor_screen, density, density_screen):
    dma = pltpu.SemaphoreType.DMA
    regular = pltpu.SemaphoreType.REGULAR
    parts = len(PARTS)
    out = pl.pallas_call(
        kernel,
        out_shape=jax.ShapeDtypeStruct((NAUX, LANES), jnp.bfloat16),
        in_specs=[pl.BlockSpec(memory_space=pltpu.HBM)] * 4,
        out_specs=pl.BlockSpec(memory_space=pltpu.VMEM),
        scratch_shapes=[
            pltpu.SMEM((1, 2), jnp.int32),
            pltpu.SMEM((1, 8), jnp.int32),
            pltpu.VMEM((SLICES, ROWS, WIDE, LANES), jnp.bfloat16),
            pltpu.VMEM((SLICES, ROWS * WIDE, LANES), jnp.float32),
            pltpu.VMEM((GROUP, ROWS, SHARE), jnp.bfloat16),
            pltpu.VMEM((DEPTH, SHARE), jnp.bfloat16),
            pltpu.VMEM((ROWS, NSIG), jnp.bfloat16),
            pltpu.VMEM((DEPTH, NSIG), jnp.bfloat16),
            pltpu.VMEM((NSIG, NSIG), jnp.bfloat16),
            pltpu.VMEM((NSIG, DEPTH), jnp.bfloat16),
            pltpu.VMEM((NSIG, SHARE), jnp.float32),
            pltpu.VMEM((NSIG, SHARE), jnp.int16),
            pltpu.VMEM((parts, 1, LANES), jnp.float32),
            pltpu.VMEM((RING - 1, SLAB, SHARE), jnp.int16),
            pltpu.VMEM((RING - 1, parts, 1, LANES), jnp.float32),
            pltpu.VMEM((SLAB, SHARE), jnp.float32),
            pltpu.VMEM((RING - 1, GROUP, SHARE), jnp.float32),
            pltpu.VMEM((8 * GROUP, LANES), jnp.float32),
            pltpu.VMEM((GROUP, 8, LANES), jnp.float32),
            pltpu.VMEM((NAUX, LANES), jnp.float32),
            pltpu.VMEM((NAUX, LANES), jnp.float32),
            dma((SLICES + 3,)), dma((parts,)),
            dma((7,)), dma((7,)),
            dma((parts, 7)), dma((parts, 7)),
            dma((parts, 7)), dma((parts, 7)),
            dma((parts, 7)), dma((parts, 7)),
            dma((parts, 7)), dma((parts, 7)),
            dma((7,)), dma((7,)),
            regular, regular, regular,
        ],
        compiler_params=pltpu.CompilerParams(
            collective_id=0, has_side_effects=True, vmem_limit_bytes=40 << 20),
        name="contract",
    )(*(pltpu.with_memory_space_constraint(v, pltpu.HBM)
        for v in (tensor_blocks, tensor_screen, density, density_screen)))
    return out.reshape(1, NAUX, LANES)


def solution(mesh):
    in_specs = (
        P(("grid", "layer"), None, None),
        P(("grid", "layer"), None),
        P(("grid", "layer"), None),
        P(("grid", "layer"), None),
    )
    out_specs = P(("grid", "layer"), None, None)
    return jax.shard_map(body, mesh=mesh, in_specs=in_specs, out_specs=out_specs, check_vma=False)
```

```python
import jax
import jax.numpy as jnp
from jax import lax
from jax.experimental import pallas as pl
from jax.experimental.pallas import tpu as pltpu
from jax.sharding import PartitionSpec as P

MESH = pl.DeviceIdType.MESH

NX, RING, CORES = 4, 8, 2
GROUP = NX * CORES
ROWS = 64
NAUX = 64
LANES = 128
NSIG = 512
SLICES = 4
WIDE = NAUX // SLICES
PARTS = 4
WIDTH = 2 * LANES
STEPS = 32000.0
TINY = 1e-33
AHEAD = 2
DEPTH = GROUP * ROWS
SLAB = GROUP * RING


def remote(src, dst, send_sem, recv_sem, device):
    return pltpu.make_async_remote_copy(
        src_ref=src, dst_ref=dst, send_sem=send_sem, recv_sem=recv_sem,
        device_id=device, device_id_type=MESH)


def kernel(tensor_hbm, tscreen_hbm, density_hbm, dscreen_hbm, out_ref,
           tscreen, dscreen, tb, tf, stage, recv_t, db, dall, perm, dt, part, coded, unit, near, units,
           first, recv_b, tiles, outgoing, fin, ordered,
           load_sem, own_sem, d_send, d_recv, t_send, t_recv,
           near_send, near_recv, unit_send, unit_recv,
           b_send, b_recv, f_send, f_recv, hello_a, hello_b, hello_far):
    grid = lax.axis_index("grid")
    z = lax.axis_index("layer")
    core = lax.rem(grid, CORES)
    y = lax.rem(grid // CORES, RING)
    x = grid // (CORES * RING)
    me = x * CORES + core

    def at(x_, y_, core_, z_):
        return ((x_ * RING + y_) * CORES + core_, z_)

    def member(pos):
        return at(pos // CORES, y, lax.rem(pos, CORES), z)

    a = jnp.where(core == 0, y, z)
    b = jnp.where(core == 0, z, y)

    def on_a(i):
        return at(x, jnp.where(core == 0, i, y), core, jnp.where(core == 0, z, i))

    def on_b(i):
        return at(x, jnp.where(core == 0, y, i), core, jnp.where(core == 0, i, z))

    def ring(i):
        return lax.rem(i + 2 * RING, RING)

    def greet(sem, peers):
        for peer in peers:
            pl.semaphore_signal(sem, inc=1, device_id=peer, device_id_type=MESH)

    load_screens = (pltpu.make_async_copy(dscreen_hbm, dscreen, load_sem.at[SLICES]),
                    pltpu.make_async_copy(tscreen_hbm, tscreen, load_sem.at[SLICES + 1]))
    load_d = pltpu.make_async_copy(density_hbm, db, load_sem.at[SLICES + 2])
    load_t = [pltpu.make_async_copy(tensor_hbm.at[:, pl.ds(c * WIDE, WIDE), :], tb.at[c], load_sem.at[c])
              for c in range(SLICES)]
    for copy in (*load_screens, load_d, *load_t):
        copy.start()

    near_a = [on_a(ring(a + 1)), on_a(ring(a - 1))]
    near_b = [on_b(ring(b + 1)), on_b(ring(b - 1))]
    far_a = [on_a(ring(a + 2)), on_a(ring(a - 2))]
    far_b = [on_b(ring(b + 2)), on_b(ring(b - 2))]
    barrier = pltpu.get_barrier_semaphore()
    peers = [member(lax.rem(me + d, GROUP)) for d in range(1, GROUP)] + near_a + near_b
    greet(barrier, peers)

    my_rows = pl.ds(pl.multiple_of(me * ROWS, ROWS), ROWS)
    lane = lax.broadcasted_iota(jnp.int32, (ROWS, LANES), 1)
    load_screens[0].wait()
    load_screens[1].wait()
    load_d.wait()
    for t in range(NSIG // LANES):
        cols = pl.ds(t * LANES, LANES)
        low = dscreen[0, 2 * t].astype(jnp.float32)
        high = dscreen[0, 2 * t + 1].astype(jnp.float32)
        keep = jnp.where(lane < 64, low, high)
        dall[my_rows, cols] = (db[:, cols].astype(jnp.float32) * keep).astype(jnp.bfloat16)

    lane = lax.broadcasted_iota(jnp.int32, (WIDE, LANES), 1)
    keep_t = jnp.where(lane < 64, tscreen[0, 0].astype(jnp.float32), tscreen[0, 1].astype(jnp.float32))

    def regroup(c):
        load_t[c].wait()

        @pl.loop(0, ROWS, unroll=16)
        def _(n):
            tf[c, pl.ds(pl.multiple_of(n * WIDE, WIDE), WIDE), :] = tb[c, n].astype(jnp.float32) * keep_t

        for pos in range(GROUP):
            for h in range(2):
                rows = tf[c, pl.ds(2 * pos + h, ROWS, stride=WIDE), :]
                stage[c, pos, :, h * LANES:(h + 1) * LANES] = rows.astype(jnp.bfloat16)

    pl.semaphore_wait(barrier, len(peers))

    other = at(x, y, 1 - core, z)
    d_copies = []
    for d in range(1, NX):
        peer = at(lax.rem(x + d, NX), y, core, z)
        d_copies.append(remote(dall.at[my_rows], dall.at[my_rows], d_send.at[d - 1], d_recv.at[d - 1], peer))
    d_copies.append(remote(dall.at[my_rows], dall.at[my_rows], d_send.at[3], d_recv.at[3], other))
    for copy in d_copies:
        copy.start()

    t_copies = {}

    def send_t(i):
        for d in range(1, GROUP):
            pos = lax.rem(me + d, GROUP)
            copy = remote(stage.at[i, pos], recv_t.at[i, my_rows], t_send.at[i, d - 1], t_recv.at[i, d - 1],
                          member(pos))
            copy.start()
            t_copies[i, d] = copy
        own = pltpu.make_async_copy(stage.at[i, me], recv_t.at[i, my_rows], own_sem.at[i])
        own.start()
        t_copies[i, 0] = own

    regroup(0)
    for i in range(1):
        send_t(i)
    greet(hello_a, near_a)
    greet(hello_b, near_b)
    for c in range(1, SLICES):
        regroup(c)

    relays = []
    for d in range(1, NX):
        d_copies[d - 1].wait_recv()
        src = lax.rem(x + NX - d, NX) * CORES + core
        rows = pl.ds(pl.multiple_of(src * ROWS, ROWS), ROWS)
        copy = remote(dall.at[rows], dall.at[rows], d_send.at[3 + d], d_recv.at[3 + d], other)
        copy.start()
        relays.append(copy)
    for i in range(1, AHEAD):
        send_t(i)

    row = lax.broadcasted_iota(jnp.int32, (SLAB, NSIG), 0)
    col = lax.broadcasted_iota(jnp.int32, (SLAB, NSIG), 1)
    j = row & 7
    for block in range(RING):
        y_ = jnp.where(core == 0, block, row >> 3)
        z_ = jnp.where(core == 0, row >> 3, block)
        sigma = (j >> 1) * 128 + y_ * 16 + (j & 1) * 8 + z_
        perm[block * SLAB:(block + 1) * SLAB, :] = jnp.where(sigma == col, 1.0, 0.0).astype(jnp.bfloat16)

    d_copies[3].wait_recv()
    for copy in relays:
        copy.wait_recv()
    dt[...] = lax.dot_general(perm[...], dall[...], (((1,), (1,)), ((), ())),
                              preferred_element_type=jnp.float32).astype(jnp.bfloat16)

    def slab(ref, i, index):
        return ref.at[i, pl.ds(pl.multiple_of(ring(index) * SLAB, SLAB), SLAB)]

    started = []

    def go(copy):
        copy.start()
        started.append(copy)
        return copy

    near_c, unit_c, b_c = {}, {}, {}

    def multiply(i):
        t_copies[i, 0].wait()
        for d in range(1, GROUP):
            t_copies[i, d].wait_recv()
        if i + AHEAD < PARTS:
            send_t(i + AHEAD)
        sums = jnp.dot(dt[...], recv_t[i], preferred_element_type=jnp.float32)
        part[i] = sums
        largest = jnp.maximum(jnp.max(jnp.abs(sums), axis=0, keepdims=True), TINY)
        unit[i] = largest * (1.0 / STEPS)
        coded[i] = jnp.round(sums * (STEPS / largest)).astype(jnp.int32).astype(jnp.int16)
        if i == 0:
            pl.semaphore_wait(hello_a, 2)
            pl.semaphore_wait(hello_b, 2)
            greet(hello_far, far_b + far_a)
            pl.semaphore_wait(hello_far, 4)
        for d in (4, 3, 5, 2, 6, 1, 7):
            unit_c[i, d] = go(remote(unit.at[i], units.at[d - 1, i], unit_send.at[i, d - 1],
                                     unit_recv.at[i, d - 1], on_a(ring(a + d))))
            near_c[i, d] = go(remote(slab(coded, i, a + d), near.at[d - 1, i], near_send.at[i, d - 1],
                                     near_recv.at[i, d - 1], on_a(ring(a + d))))

    def reduce_a(i):
        total = slab(part, i, a)[...]
        for d in range(1, RING):
            near_c[i, d].wait_recv()
            unit_c[i, d].wait_recv()
            total = total + near[d - 1, i].astype(jnp.int32).astype(jnp.float32) * units[d - 1, i]
        first[i] = total
        for d in range(1, RING):
            to = ring(b + d)
            rows = pl.ds(pl.multiple_of(to * GROUP, GROUP), GROUP)
            b_c[i, d] = go(remote(first.at[i, rows], recv_b.at[d - 1, i], b_send.at[i, d - 1],
                                  b_recv.at[i, d - 1], on_b(to)))

    def reduce_b(i):
        rows = pl.ds(pl.multiple_of(b * GROUP, GROUP), GROUP)
        total = first[i, rows, :]
        for d in range(1, RING):
            b_c[i, d].wait_recv()
            total = total + recv_b[d - 1, i]
        for h in range(2):
            q = 2 * i + h
            tiles[q * GROUP:(q + 1) * GROUP, :] = total[:, h * LANES:(h + 1) * LANES]

    last = PARTS
    for step in range(last + 4):
        if step < last:
            multiply(step)
        if 0 <= step - 2 < last:
            reduce_a(step - 2)
        if 0 <= step - 4 < last:
            reduce_b(step - 4)

    for k in range(GROUP):
        outgoing[k] = tiles[pl.ds(k, 8, stride=GROUP), :]
    mine = pl.ds(pl.multiple_of(me * 8, 8), 8)
    f_c = []
    for d in range(1, GROUP):
        pos = lax.rem(me + d, GROUP)
        copy = remote(outgoing.at[pos], fin.at[mine], f_send.at[d - 1], f_recv.at[d - 1], member(pos))
        copy.start()
        f_c.append(copy)
    fin[mine, :] = outgoing[me]
    for copy in d_copies + relays + started:
        copy.wait_send()
    for i in range(last):
        for d in range(1, GROUP):
            t_copies[i, d].wait_send()
    for copy in f_c:
        copy.wait()
    for q in range(8):
        ordered[pl.ds(WIDE * (q // 2) + q % 2, GROUP, stride=2), :] = fin[pl.ds(q, GROUP, stride=8), :]
    out_ref[...] = ordered[...].astype(jnp.bfloat16)


def body(tensor_blocks, tensor_screen, density, density_screen):
    dma = pltpu.SemaphoreType.DMA
    regular = pltpu.SemaphoreType.REGULAR
    parts = PARTS
    out = pl.pallas_call(
        kernel,
        out_shape=jax.ShapeDtypeStruct((NAUX, LANES), jnp.bfloat16),
        in_specs=[pl.BlockSpec(memory_space=pltpu.HBM)] * 4,
        out_specs=pl.BlockSpec(memory_space=pltpu.VMEM),
        scratch_shapes=[
            pltpu.SMEM((1, 2), jnp.int32),
            pltpu.SMEM((1, 8), jnp.int32),
            pltpu.VMEM((SLICES, ROWS, WIDE, LANES), jnp.bfloat16),
            pltpu.VMEM((SLICES, ROWS * WIDE, LANES), jnp.float32),
            pltpu.VMEM((parts, GROUP, ROWS, WIDTH), jnp.bfloat16),
            pltpu.VMEM((parts, DEPTH, WIDTH), jnp.bfloat16),
            pltpu.VMEM((ROWS, NSIG), jnp.bfloat16),
            pltpu.VMEM((DEPTH, NSIG), jnp.bfloat16),
            pltpu.VMEM((NSIG, NSIG), jnp.bfloat16),
            pltpu.VMEM((NSIG, DEPTH), jnp.bfloat16),
            pltpu.VMEM((parts, NSIG, WIDTH), jnp.float32),
            pltpu.VMEM((parts, NSIG, WIDTH), jnp.int16),
            pltpu.VMEM((parts, 1, WIDTH), jnp.float32),
            pltpu.VMEM((RING - 1, parts, SLAB, WIDTH), jnp.int16),
            pltpu.VMEM((RING - 1, parts, 1, WIDTH), jnp.float32),
            pltpu.VMEM((parts, SLAB, WIDTH), jnp.float32),
            pltpu.VMEM((RING - 1, parts, GROUP, WIDTH), jnp.float32),
            pltpu.VMEM((8 * GROUP, LANES), jnp.float32),
            pltpu.VMEM((GROUP, 8, LANES), jnp.float32),
            pltpu.VMEM((NAUX, LANES), jnp.float32),
            pltpu.VMEM((NAUX, LANES), jnp.float32),
            dma((SLICES + 3,)), dma((parts,)),
            dma((7,)), dma((7,)),
            dma((parts, 7)), dma((parts, 7)),
            dma((parts, 7)), dma((parts, 7)),
            dma((parts, 7)), dma((parts, 7)),
            dma((parts, 7)), dma((parts, 7)),
            dma((7,)), dma((7,)),
            regular, regular, regular,
        ],
        compiler_params=pltpu.CompilerParams(
            collective_id=0, has_side_effects=True, vmem_limit_bytes=40 << 20),
        name="contract",
    )(*(pltpu.with_memory_space_constraint(v, pltpu.HBM)
        for v in (tensor_blocks, tensor_screen, density, density_screen)))
    return out.reshape(1, NAUX, LANES)


def solution(mesh):
    in_specs = (
        P(("grid", "layer"), None, None),
        P(("grid", "layer"), None),
        P(("grid", "layer"), None),
        P(("grid", "layer"), None),
    )
    out_specs = P(("grid", "layer"), None, None)
    return jax.shard_map(body, mesh=mesh, in_specs=in_specs, out_specs=out_specs, check_vma=False)
```
